256 devices in a mesh: row: 16 (over y_hi, z), col: 16 (over x, y_lo, core).
Axes of the slice: x: 4, y: 4 (y_hi: 2, y_lo: 2; y = y_hi * 2 + y_lo), z: 8, core: 2. Of those that a mesh axis runs over, the one named last changes fastest.
Arguments:
- inputs: bfloat16 [2048, 6144], P('col', 'row'), may hold values from -6 to 6
- out_grad: bfloat16 [2048, 6144], P('col', 'row'), may hold values from -6 to 6
- preact: bfloat16 [2048, 24576], P('row', 'col'), may hold values from -6 to 6
- w_in: bfloat16 [6144, 24576], P('row', 'col'), may hold values from -0.078125 to 0.078125
- w_out: bfloat16 [24576, 6144], P('col', 'row'), may hold values from -0.0390625 to 0.0390625
Outputs:
- input_grad: bfloat16 [2048, 6144], P('col', 'row')
- w_in_grad: float32 [6144, 24576], P('row', 'col')
- w_out_grad: float32 [24576, 6144], P('col', 'row')
The draws below stay inside these ranges and needn't reach their ends.
All inputs are finite; a program needn't handle non-finite values.
Results may differ from the reference program's by a relative error of at most 0.005.
Values may be sent and summed in bfloat16 or wider, within the bound.
No kernel may reach another device: no remote copies, remote signals or barrier semaphores. Data moves between devices by JAX's collectives and lax.ppermute only.
A program may use at most 128 MiB of HBM per device.

```python
import jax
import jax.numpy as jnp
from jax import lax

D = 6144
FF = 24576
TOKENS = 2048


def strengthened(result, rng, source, target, parts, factor):
    def block_of(position):
        return (jnp.arange(result.shape[position]) // (result.shape[position] // parts)).reshape((-1,) + (1,) * (result.ndim - 1 - position))

    one_side = jax.random.permutation(rng, parts)[block_of(target)]
    second = (block_of(target) + parts // 2) % parts
    return jnp.where((block_of(source) == one_side) | (block_of(source) == second), factor * result, result)


def levels(stream_key, dims, cuts, least, high):
    gain, own = 1.0, jax.random.fold_in(stream_key, 6)
    for position, shards_of in cuts:
        heights = jnp.exp(jax.random.uniform(jax.random.fold_in(own, position), (shards_of,), jnp.float32, least / len(cuts), high / len(cuts)))
        gain = gain * jnp.repeat(heights, dims[position] // shards_of).reshape([-1 if axis == position else 1 for axis in range(len(dims))])
    return gain


def noise(rng, shape, width, reach, pieces=(), kind=jnp.bfloat16):
    loudness = levels(rng, shape, pieces, -0.22, 0.18) if pieces else 1.0
    entries = jax.random.normal(rng, shape, jnp.float32) * width * loudness
    return jnp.minimum(jnp.maximum(entries, -reach), reach).astype(kind)


def heavy_noise(rng, dims, deviation, limit, cuts, heavy, dtype=jnp.bfloat16):
    array = deviation * jax.random.normal(rng, dims, jnp.float32)
    if cuts:
        array = array * levels(rng, dims, cuts, -0.22, 0.18)
    return jnp.clip(strengthened(array, jax.random.fold_in(rng, 3), *heavy), -limit, limit).astype(dtype)


def setup_inputs(seed: int = 0) -> dict:
    streams_of = jax.random.split(jax.random.key(seed), 6)
    inputs = noise(streams_of[0], (TOKENS, D), 1.0, 6.0, ((0, 16), (1, 16)))
    out_grad = heavy_noise(streams_of[1], (TOKENS, D), 1.0, 6.0, ((0, 16), (1, 16)), (1, 0, 16, 2.0))
    preact = noise(streams_of[2], (TOKENS, FF), 1.5, 6.0, ((0, 16), (1, 16)))
    w_in = noise(streams_of[3], (D, FF), D ** -0.5, 0.078125, ((0, 16), (1, 16)))
    w_out = noise(streams_of[4], (FF, D), FF ** -0.5, 0.0390625, ((0, 16), (1, 16)))
    return {"inputs": inputs, "out_grad": out_grad, "preact": preact, "w_in": w_in, "w_out": w_out}


def gelu_value(z):
    inner = 0.7978845608 * (z + 0.044715 * z * z * z)
    return 0.5 * z * (1.0 + jnp.tanh(inner))


def gelu_slope(z):
    inner = 0.7978845608 * (z + 0.044715 * z * z * z)
    tangent = jnp.tanh(inner)
    return 0.5 * (1.0 + tangent) + 0.5 * z * (1.0 - tangent * tangent) * 0.7978845608 * (1.0 + 3.0 * 0.044715 * z * z)


def reference(inputs, out_grad, preact, w_in, w_out):
    pre_float = preact.astype(jnp.float32)
    hidden = gelu_value(pre_float).astype(jnp.bfloat16)
    hidden_grad = lax.dot_general(out_grad, w_out, (((1,), (1,)), ((), ())), preferred_element_type=jnp.float32)
    preact_grad = (hidden_grad * gelu_slope(pre_float)).astype(jnp.bfloat16)
    w_out_grad = lax.dot_general(hidden, out_grad, (((0,), (0,)), ((), ())), preferred_element_type=jnp.float32)
    w_in_grad = lax.dot_general(inputs, preact_grad, (((0,), (0,)), ((), ())), preferred_element_type=jnp.float32)
    input_grad = lax.dot_general(preact_grad, w_in, (((1,), (1,)), ((), ())), preferred_element_type=jnp.float32)
    return input_grad.astype(jnp.bfloat16), w_in_grad, w_out_grad
```

```python
import functools

import jax
import jax.numpy as jnp
from jax import lax
from jax.experimental import pallas as pl
from jax.experimental.pallas import tpu as pltpu
from jax.sharding import Mesh, PartitionSpec as P

BF = jnp.bfloat16
F32 = jnp.float32
RING = 8


def gelu_value(z):
    inner = 0.7978845608 * (z + 0.044715 * z * z * z)
    return 0.5 * z * (1.0 + jnp.tanh(inner))


def gelu_slope(z):
    inner = 0.7978845608 * (z + 0.044715 * z * z * z)
    tangent = jnp.tanh(inner)
    return 0.5 * (1.0 + tangent) + 0.5 * z * (1.0 - tangent * tangent) * 0.7978845608 * (
        1.0 + 3.0 * 0.044715 * z * z
    )


def up(a):
    return lax.ppermute(a, "z", [(i, (i + 1) % RING) for i in range(RING)])


def down(a):
    return lax.ppermute(a, "z", [(i, (i - 1) % RING) for i in range(RING)])


def swap_h(a):
    return lax.ppermute(a, "h", [(0, 1), (1, 0)])


def swap_c(a):
    return lax.ppermute(a, "c", [(0, 1), (1, 0)])


def swap_x(a, d):
    return lax.ppermute(a, "x", [(i, i ^ d) for i in range(4)])


def swap_y(a, d):
    return lax.ppermute(a, ("h", "yl"), [(i, i ^ d) for i in range(4)])


def dot(a, b, ca, cb):
    return lax.dot_general(a, b, (((ca,), (cb,)), ((), ())), preferred_element_type=F32)


ANY = pl.BlockSpec(memory_space=pl.ANY)
SCALARS = pl.BlockSpec(memory_space=pltpu.SMEM)


def panel_kernel(where, *refs):
    pieces, panel, sems = refs[:8], refs[8], refs[9]
    width = pieces[0].shape[3]
    copies = []
    for dx in range(4):
        for dc in range(2):
            for dyl in range(2):
                place = where[((dx & 1) * 2 + dyl) * 2 + dc]
                for dh in range(2):
                    copies.append(
                        pltpu.make_async_copy(
                            pieces[dx * 2 + dc].at[dyl, dh],
                            panel.at[place, dx >> 1, :, pl.ds(dh * width, width)],
                            sems.at[len(copies)],
                        )
                    )
    for copy in copies:
        copy.start()
    for copy in copies:
        copy.wait()


def panel_of(where, pieces):
    tokens, width = pieces[0].shape[2:]
    return pl.pallas_call(
        panel_kernel,
        out_shape=jax.ShapeDtypeStruct((8, 2, tokens, 2 * width), BF),
        in_specs=[SCALARS] + [ANY] * 8,
        out_specs=ANY,
        scratch_shapes=[pltpu.SemaphoreType.DMA((32,))],
        cost_estimate=pl.CostEstimate(flops=0, bytes_accessed=64 * tokens * width * 2, transcendentals=0),
        name="panel",
    )(where, *pieces)


def reorder_kernel(where, *refs):
    chunks, out, sems = refs[:8], refs[8], refs[9]
    copies = [pltpu.make_async_copy(chunks[k], out.at[where[k]], sems.at[k]) for k in range(8)]
    for copy in copies:
        copy.start()
    for copy in copies:
        copy.wait()


def reordered(where, chunks):
    shape = chunks[0].shape
    return pl.pallas_call(
        reorder_kernel,
        out_shape=jax.ShapeDtypeStruct((8,) + shape, BF),
        in_specs=[SCALARS] + [ANY] * 8,
        out_specs=ANY,
        scratch_shapes=[pltpu.SemaphoreType.DMA((8,))],
        cost_estimate=pl.CostEstimate(flops=0, bytes_accessed=32 * shape[0] * shape[1], transcendentals=0),
        name="reorder",
    )(where, *chunks)


def slab_gather(a):
    own = jnp.stack([jnp.stack([a, swap_y(a, 2)]), jnp.stack([swap_y(a, 1), swap_y(a, 3)])])
    by_x = [own] + [swap_x(own, d) for d in (1, 2, 3)]
    pieces = []
    for piece in by_x:
        pieces += [piece, swap_c(piece)]
    return pieces


def local(inputs, out_grad, preact, w_in, w_out):
    h, z, x = lax.axis_index("h"), lax.axis_index("z"), lax.axis_index("x")
    yl, c = lax.axis_index("yl"), lax.axis_index("c")
    low = (x & 1) * 4 + yl * 2 + c
    ks = jnp.arange(8, dtype=jnp.int32)
    place_of = ((ks ^ low) - z) & 7
    diff_of = low ^ ((z + ks) & 7)
    slot_of = (diff_of & 1) * 4 + (diff_of >> 1)
    half = preact.shape[1] // 2
    tokens, width = out_grad.shape

    def halves(a, axis):
        first, second = lax.slice_in_dim(a, 0, half, axis=axis), lax.slice_in_dim(a, half, 2 * half, axis=axis)
        return jnp.where(h == 0, first, second), jnp.where(h == 0, second, first)

    pre_own, pre_send = halves(preact, 1)
    pre_recv = swap_h(pre_send)
    grad_pieces = slab_gather(out_grad)
    pre_a = jnp.where(h == (x >> 1), pre_own, pre_recv).astype(F32)
    pre_b = jnp.where(h == (x >> 1), pre_recv, pre_own).astype(F32)
    pre = jnp.concatenate([pre_a, pre_b], axis=0)
    hidden = gelu_value(pre).astype(BF)
    slope = (gelu_slope(pre_a), gelu_slope(pre_b))

    wo_own, wo_send = halves(w_out, 0)
    w_out2 = jnp.concatenate([wo_own, swap_h(wo_send)], axis=1)
    wi_own, wi_send = halves(w_in, 1)
    w_in2 = jnp.concatenate([wi_own, swap_h(wi_send)], axis=0)

    def gather_ring(a, more_up):
        out = [a] + [None] * 7
        u = d = a
        for step in range(1, 5):
            if step < 4 or more_up:
                u = up(u)
                out[8 - step] = u
            if step < 4 or not more_up:
                d = down(d)
                out[step] = d
        return out

    hidden_chunks = gather_ring(hidden, True)

    panel = panel_of(place_of, grad_pieces)

    def part(k, s):
        return dot(panel[k, s], w_out2, 1, 1)

    local_grads = []
    for s in range(2):
        far_up = 4 if s == 0 else 3
        run_up = part(far_up, s)
        run_down = part(8 - (7 - far_up), s)
        for k in range(far_up - 1, -1, -1):
            got = up(run_up.astype(BF)).astype(F32)
            run_up = part(k, s) + got if k else got
        for k in range(7 - far_up - 1, -1, -1):
            got = down(run_down.astype(BF)).astype(F32)
            run_down = part(8 - k, s) + got if k else got
        local_grads.append(((part(0, s) + run_up + run_down) * slope[s]).astype(BF))

    grads = [gather_ring(local_grads[0], True), gather_ring(local_grads[1], False)]

    hidden_all = jnp.concatenate(hidden_chunks, axis=0)
    panel_all = panel.reshape(16 * tokens, 2 * width)
    wo_other = swap_h(dot(hidden_all, panel_all[:, width:], 0, 0).astype(BF)).astype(F32)
    wo_mine = dot(hidden_all, panel_all[:, :width], 0, 0)
    w_out_grad = jnp.where(
        h == 0, jnp.concatenate([wo_mine, wo_other], axis=0), jnp.concatenate([wo_other, wo_mine], axis=0)
    )

    slab = lax.all_gather(inputs, ("h", "x", "yl", "c"), axis=0)
    slab = slab.reshape(2, 2, 8, tokens, width)
    order = (z + ks) & 7
    swapped = jnp.where(x >> 1 == 0, slab, slab[:, ::-1])
    swapped = jnp.where(h == 0, swapped, swapped[::-1])
    rolled = jnp.concatenate([swapped, swapped[:, :, :7]], axis=2)
    rolled = lax.dynamic_slice_in_dim(rolled, z, 8, axis=2)
    input_all = rolled.transpose(2, 1, 3, 0, 4).reshape(16 * tokens, 2 * width)

    chunk_grads = [jnp.concatenate([grads[0][k], grads[1][k]], axis=0) for k in range(8)]
    partial = [dot(g, w_in2, 1, 1).astype(BF) for g in chunk_grads]
    split = reordered(slot_of, partial)
    keep, send = split[:4], split[4:]
    total = keep.astype(F32) + swap_c(send).astype(F32)
    total = total.reshape(2, 2, 2, tokens, 2 * width)
    by_x = total[0, :, 0]
    for d in (1, 2, 3):
        by_x = by_x + swap_x(total[d & 1, :, d >> 1].astype(BF), d).astype(F32)
    by_y = by_x[0, :, :width]
    by_y = by_y + swap_y(by_x[1, :, :width].astype(BF), 1).astype(F32)
    by_y = by_y + swap_y(by_x[0, :, width:].astype(BF), 2).astype(F32)
    by_y = by_y + swap_y(by_x[1, :, width:].astype(BF), 3).astype(F32)
    input_grad = by_y.astype(BF)

    grad_all = jnp.concatenate(chunk_grads, axis=0)
    wi_other = swap_h(dot(input_all[:, width:], grad_all, 0, 0).astype(BF)).astype(F32)
    wi_mine = dot(input_all[:, :width], grad_all, 0, 0)
    w_in_grad = jnp.where(
        h == 0, jnp.concatenate([wi_mine, wi_other], axis=1), jnp.concatenate([wi_other, wi_mine], axis=1)
    )
    return input_grad, w_in_grad, w_out_grad


def solution(mesh):
    fine = Mesh(mesh.devices.reshape(2, RING, 4, 2, 2), ("h", "z", "x", "yl", "c"))
    col, row = ("x", "yl", "c"), ("h", "z")
    in_specs = (P(col, row), P(col, row), P(row, col), P(row, col), P(col, row))
    out_specs = (P(col, row), P(row, col), P(col, row))
    return jax.shard_map(local, mesh=fine, in_specs=in_specs, out_specs=out_specs, check_vma=False)
```

```python
import functools

import jax
import jax.numpy as jnp
from jax import lax
from jax.experimental import pallas as pl
from jax.experimental.pallas import tpu as pltpu
from jax.sharding import Mesh, PartitionSpec as P

BF = jnp.bfloat16
F32 = jnp.float32
RING = 8
VMEM_GRANT = 48 * 1024 * 1024


def gelu_value(z):
    inner = 0.7978845608 * (z + 0.044715 * z * z * z)
    return 0.5 * z * (1.0 + jnp.tanh(inner))


def gelu_slope(z):
    inner = 0.7978845608 * (z + 0.044715 * z * z * z)
    tangent = jnp.tanh(inner)
    return 0.5 * (1.0 + tangent) + 0.5 * z * (1.0 - tangent * tangent) * 0.7978845608 * (
        1.0 + 3.0 * 0.044715 * z * z
    )


def up(a):
    return lax.ppermute(a, "z", [(i, (i + 1) % RING) for i in range(RING)])


def down(a):
    return lax.ppermute(a, "z", [(i, (i - 1) % RING) for i in range(RING)])


def swap_h(a):
    return lax.ppermute(a, "h", [(0, 1), (1, 0)])


def swap_c(a):
    return lax.ppermute(a, "c", [(0, 1), (1, 0)])


def swap_x(a, d):
    return lax.ppermute(a, "x", [(i, i ^ d) for i in range(4)])


def swap_y(a, d):
    return lax.ppermute(a, ("h", "yl"), [(i, i ^ d) for i in range(4)])


def together(*arrays):
    return lax.optimization_barrier(arrays)


def after(a, *others):
    return lax.optimization_barrier((a,) + others)[0]


def dot(a, b, ca, cb):
    return lax.dot_general(a, b, (((ca,), (cb,)), ((), ())), preferred_element_type=F32)


ANY = pl.BlockSpec(memory_space=pl.ANY)
SCALARS = pl.BlockSpec(memory_space=pltpu.SMEM)
WHOLE = pl.BlockSpec(memory_space=pltpu.VMEM)


def assemble(moves, where, pieces, shape, name):
    def kernel(where_ref, *refs):
        panel, sems = refs[-2], refs[-1]
        copies = [
            pltpu.make_async_copy(source, place, sems.at[n])
            for n, (source, place) in enumerate(moves(where_ref, refs[:-2], panel))
        ]
        for copy in copies:
            copy.start()
        for copy in copies:
            copy.wait()

    size = pieces[0].dtype.itemsize
    for length in shape:
        size *= length
    return pl.pallas_call(
        kernel,
        out_shape=jax.ShapeDtypeStruct(shape, pieces[0].dtype),
        in_specs=[SCALARS] + [ANY] * len(pieces),
        out_specs=WHOLE,
        scratch_shapes=[pltpu.SemaphoreType.DMA((32,))],
        compiler_params=pltpu.CompilerParams(vmem_limit_bytes=VMEM_GRANT),
        cost_estimate=pl.CostEstimate(flops=0, bytes_accessed=3 * size, transcendentals=0),
        name=name,
    )(where, *pieces)


def panel_moves(where, pieces, panel):
    width = pieces[0].shape[3]
    for dx in range(4):
        for dc in range(2):
            for dyl in range(2):
                place = where[((dx & 1) * 2 + dyl) * 2 + dc]
                for dh in range(2):
                    yield (
                        pieces[dx * 2 + dc].at[dyl, dh],
                        panel.at[place, dx >> 1, :, pl.ds(dh * width, width)],
                    )


def slab_moves(where, pieces, panel):
    width = pieces[0].shape[2]
    for k in range(8):
        for dx2 in range(2):
            for dh in range(2):
                yield (
                    pieces[0].at[where[(k * 2 + dx2) * 2 + dh]],
                    panel.at[k, dx2, :, pl.ds(dh * width, width)],
                )


def stack_moves(where, pieces, panel):
    rows = pieces[0].shape[0]
    for n, piece in enumerate(pieces):
        yield piece, panel.at[pl.ds(n * rows, rows)]


def roll_moves(where, pieces, panel):
    for k in range(8):
        yield pieces[0].at[where[k]], panel.at[k]


def head(where, pieces, weights):
    tokens, width = pieces[0].shape[2:]
    half = weights.shape[0]

    def kernel(where_ref, *refs):
        weights_ref, panel, outs, sems = refs[8], refs[9], refs[10:12], refs[12]
        copies = [
            pltpu.make_async_copy(source, place, sems.at[n])
            for n, (source, place) in enumerate(panel_moves(where_ref, refs[:8], panel))
        ]
        for copy in copies:
            copy.start()
        for copy in copies:
            copy.wait()
        for out, k in zip(outs, (4, 5)):
            rows = panel[k].reshape(2 * tokens, 2 * width)
            out[...] = dot(rows, weights_ref[...], 1, 1).astype(BF)

    return pl.pallas_call(
        kernel,
        out_shape=[jax.ShapeDtypeStruct((8, 2, tokens, 2 * width), BF)]
        + [jax.ShapeDtypeStruct((2 * tokens, half), BF)] * 2,
        in_specs=[SCALARS] + [ANY] * 8 + [WHOLE],
        out_specs=[WHOLE] * 3,
        scratch_shapes=[pltpu.SemaphoreType.DMA((32,))],
        compiler_params=pltpu.CompilerParams(vmem_limit_bytes=VMEM_GRANT),
        cost_estimate=pl.CostEstimate(flops=16 * tokens * width * half, bytes_accessed=96 * tokens * width, transcendentals=0),
        name="head",
    )(where, *pieces, weights)


def spread(where, pieces):
    tokens, width = pieces[0].shape[0] // 2, pieces[0].shape[1]

    def kernel(where_ref, *refs):
        sums, parts, total = refs[:8], refs[8:12], refs[12]
        for n in range(8):
            total[where_ref[n]] = sums[n][...]
        for d in range(4):
            for dyl in range(2):
                for dc in range(2):
                    part = total[((d & 1) * 2 + dyl) * 2 + dc, pl.ds((d >> 1) * tokens, tokens)]
                    parts[d][dyl, dc] = part.astype(parts[d].dtype)

    return pl.pallas_call(
        kernel,
        out_shape=[jax.ShapeDtypeStruct((2, 2, tokens, width), BF if d else F32) for d in range(4)],
        in_specs=[SCALARS] + [WHOLE] * 8,
        out_specs=[WHOLE] * 4,
        scratch_shapes=[pltpu.VMEM((8, 2 * tokens, width), F32)],
        compiler_params=pltpu.CompilerParams(vmem_limit_bytes=VMEM_GRANT),
        cost_estimate=pl.CostEstimate(flops=0, bytes_accessed=104 * tokens * width, transcendentals=0),
        name="spread",
    )(where, *pieces)


def local(inputs, out_grad, preact, w_in, w_out):
    h, z, x = lax.axis_index("h"), lax.axis_index("z"), lax.axis_index("x")
    yl, c = lax.axis_index("yl"), lax.axis_index("c")
    low = (x & 1) * 4 + yl * 2 + c
    ks = jnp.arange(8, dtype=jnp.int32)
    place_of = ((ks ^ low) - z) & 7
    half = preact.shape[1] // 2
    tokens, width = out_grad.shape

    def halves(a, axis):
        return (
            lax.dynamic_slice_in_dim(a, h * half, half, axis=axis),
            lax.dynamic_slice_in_dim(a, (1 - h) * half, half, axis=axis),
        )

    pre_own, pre_send = halves(preact, 1)
    y1, y2, y3, pre_recv = together(swap_y(out_grad, 1), swap_y(out_grad, 2), swap_y(out_grad, 3), swap_h(pre_send))
    own = jnp.stack([jnp.stack([out_grad, y2]), jnp.stack([y1, y3])])
    wo_own, wo_send = halves(w_out, 0)
    wi_own, wi_send = halves(w_in, 1)
    wo_send, wi_send = after(wo_send, own), after(wi_send, own)
    by_x = [own] + [swap_x(own, d) for d in (1, 2, 3)]
    grad_pieces = []
    for piece in by_x:
        grad_pieces += [piece, swap_c(piece)]
    w_out2 = jnp.concatenate([wo_own, swap_h(wo_send)], axis=1)

    pre = jnp.where(
        h == (x >> 1), jnp.concatenate([pre_own, pre_recv], axis=0), jnp.concatenate([pre_recv, pre_own], axis=0)
    ).astype(F32)
    hidden = gelu_value(pre).astype(BF)
    slope = gelu_slope(pre)
    hidden_slab = lax.all_gather(hidden, "z", axis=0)
    inputs, _ = together(inputs, hidden)
    slab = lax.all_gather(inputs, ("h", "x", "yl", "c"), axis=0)

    wi_other = swap_h(wi_send)

    panel, run_up, run_down = head(place_of, grad_pieces, w_out2)
    panel_all = panel.reshape(16 * tokens, 2 * width)
    parts = dot(panel_all, w_out2, 1, 1).reshape(8, 2 * tokens, half)

    def add(part, got):
        return (part + got.astype(F32)).astype(BF)

    run_up, run_down, wi_other = together(run_up, run_down, wi_other)
    run_up, run_down = up(run_up), down(run_down)
    w_in_keep = jnp.where(c == 0, wi_own, wi_other)
    w_in_send = jnp.where(c == 0, wi_other, wi_own)
    run_up, run_down = together(add(parts[3], run_up), add(parts[6], run_down))
    run_up, run_down = up(run_up), down(run_down)
    run_up, run_down = together(add(parts[2], run_up), add(parts[7], run_down))
    run_up, run_down = up(run_up), down(run_down)
    hidden_all = assemble(roll_moves, (z + ks) & 7, [hidden_slab], (8, 2 * tokens, half), "hidden_panel")
    hidden_all = hidden_all.reshape(16 * tokens, half)
    run_up = up(add(parts[1], run_up))
    run_up, run_down, hidden_all, w_in_keep, w_in_send = together(run_up, run_down, hidden_all, w_in_keep, w_in_send)
    total = parts[0] + run_down.astype(F32) + run_up.astype(F32)

    g = [None] * 8
    g[0] = (total * slope).astype(BF)

    def both_cores(chunk):
        got = swap_c(dot(chunk, w_in_send, 1, 1).astype(BF))
        return dot(chunk, w_in_keep, 1, 1) + got.astype(F32)

    sums = [None] * 8
    g[7], g[1] = up(g[0]), down(g[0])
    wo_other = dot(hidden_all, panel_all[:, width:], 0, 0).astype(BF)
    g[7], g[1], wo_other = together(g[7], g[1], wo_other)
    g[6], g[2] = up(g[7]), down(g[1])
    wo_other = swap_h(wo_other)
    sums[0] = both_cores(after(g[0], g[7]))
    sums[1], sums[7] = both_cores(g[1]), both_cores(g[7])
    g[6], g[2], sums[0], sums[1], sums[7] = together(g[6], g[2], sums[0], sums[1], sums[7])
    g[5], g[3] = up(g[6]), down(g[2])
    sums[2], sums[6] = both_cores(g[2]), both_cores(g[6])
    hidden_all = after(hidden_all, g[6])
    wo_mine = dot(hidden_all, panel_all[:, :width], 0, 0)
    g[5], sums[2], sums[6], wo_mine = together(g[5], sums[2], sums[6], wo_mine)
    g[4] = up(g[5])
    sums[3], sums[5] = both_cores(g[3]), both_cores(g[5])
    n = jnp.arange(32, dtype=jnp.int32)
    k = jnp.array([0, 1, 2, 3, 5, 6, 7, 4], jnp.int32)[n >> 2]
    owner = (((n & 1) ^ h) * 2 + (((n >> 1) & 1) ^ (x >> 1))) * 8 + ((z + k) & 7)
    slab = after(slab, g[5])
    input_all = assemble(slab_moves, owner, [slab], (8, 2, tokens, 2 * width), "input_panel")
    input_all = input_all.reshape(16 * tokens, 2 * width)
    early = 14 * tokens
    grad_early = assemble(stack_moves, ks, g[:4] + g[5:], (early, half), "preact_panel")
    wi_send = dot(input_all[:early, width:], grad_early, 0, 0)
    g[4], sums[3], sums[5], wi_send = together(g[4], sums[3], sums[5], wi_send)
    sums[4] = both_cores(g[4])
    wi_send = (wi_send + dot(input_all[early:, width:], g[4], 0, 0)).astype(BF)
    wi_other = swap_h(wi_send)
    sums[4] = after(sums[4], wi_send)
    slot_of = low ^ ((z + ks) & 7)
    by_x, *others = spread(slot_of, sums)
    others = [swap_x(others[d - 1], d) for d in (1, 2, 3)]

    wo_other, g[4], grad_early = after(wo_other, by_x), after(g[4], by_x), after(grad_early, by_x)
    wi_mine = dot(input_all[:early, :width], grad_early, 0, 0) + dot(input_all[early:, :width], g[4], 0, 0)
    w_out_grad = jnp.where(
        h == 0,
        jnp.concatenate([wo_mine, wo_other.astype(F32)], axis=0),
        jnp.concatenate([wo_other.astype(F32), wo_mine], axis=0),
    )
    others[1], wi_mine, w_out_grad = together(others[1], wi_mine, w_out_grad)

    for part in others:
        by_x = by_x + part.astype(F32)
    to_first = [(i, i ^ 2) if i % 2 == 0 else (i, i ^ 6) for i in range(8)]
    to_second = [(i, i ^ 4) for i in range(1, 8, 2)]
    moved, wi_other = together(by_x.astype(BF), wi_other)
    got = lax.ppermute(moved[1], ("h", "yl", "c"), to_first).astype(F32)
    got_second = lax.ppermute(moved[0], ("h", "yl", "c"), to_second).astype(F32)
    by_y = got + jnp.where(c == 0, by_x[0], got_second)
    by_y = by_y[0] + swap_c(by_y[1])
    input_grad = by_y.astype(BF)
    w_in_grad = jnp.where(
        h == 0,
        jnp.concatenate([wi_mine, wi_other.astype(F32)], axis=1),
        jnp.concatenate([wi_other.astype(F32), wi_mine], axis=1),
    )
    return input_grad, w_in_grad, w_out_grad


def solution(mesh):
    fine = Mesh(mesh.devices.reshape(2, RING, 4, 2, 2), ("h", "z", "x", "yl", "c"))
    col, row = ("x", "yl", "c"), ("h", "z")
    in_specs = (P(col, row), P(col, row), P(row, col), P(row, col), P(col, row))
    out_specs = (P(col, row), P(row, col), P(col, row))
    return jax.shard_map(local, mesh=fine, in_specs=in_specs, out_specs=out_specs, check_vma=False)
```

```python
import functools

import jax
import jax.numpy as jnp
from jax import lax
from jax.experimental import pallas as pl
from jax.experimental.pallas import tpu as pltpu
from jax.sharding import Mesh, PartitionSpec as P

BF = jnp.bfloat16
F32 = jnp.float32
RING = 8
VMEM_GRANT = 48 * 1024 * 1024


def gelu_value(z):
    inner = 0.7978845608 * (z + 0.044715 * z * z * z)
    return 0.5 * z * (1.0 + jnp.tanh(inner))


def gelu_slope(z):
    inner = 0.7978845608 * (z + 0.044715 * z * z * z)
    tangent = jnp.tanh(inner)
    return 0.5 * (1.0 + tangent) + 0.5 * z * (1.0 - tangent * tangent) * 0.7978845608 * (
        1.0 + 3.0 * 0.044715 * z * z
    )


def up(a):
    return lax.ppermute(a, "z", [(i, (i + 1) % RING) for i in range(RING)])


def down(a):
    return lax.ppermute(a, "z", [(i, (i - 1) % RING) for i in range(RING)])


def swap_h(a):
    return lax.ppermute(a, "h", [(0, 1), (1, 0)])


def swap_c(a):
    return lax.ppermute(a, "c", [(0, 1), (1, 0)])


def swap_x(a, d):
    return lax.ppermute(a, "x", [(i, i ^ d) for i in range(4)])


def swap_y(a, d):
    return lax.ppermute(a, ("h", "yl"), [(i, i ^ d) for i in range(4)])


def together(*arrays):
    return lax.optimization_barrier(arrays)


def after(a, *others):
    return lax.optimization_barrier((a,) + others)[0]


def dot(a, b, ca, cb):
    return lax.dot_general(a, b, (((ca,), (cb,)), ((), ())), preferred_element_type=F32)


ANY = pl.BlockSpec(memory_space=pl.ANY)
SCALARS = pl.BlockSpec(memory_space=pltpu.SMEM)
WHOLE = pl.BlockSpec(memory_space=pltpu.VMEM)


def assemble(moves, where, pieces, shape, name):
    def kernel(where_ref, *refs):
        panel, sems = refs[-2], refs[-1]
        copies = [
            pltpu.make_async_copy(source, place, sems.at[n])
            for n, (source, place) in enumerate(moves(where_ref, refs[:-2], panel))
        ]
        for copy in copies:
            copy.start()
        for copy in copies:
            copy.wait()

    size = pieces[0].dtype.itemsize
    for length in shape:
        size *= length
    return pl.pallas_call(
        kernel,
        out_shape=jax.ShapeDtypeStruct(shape, pieces[0].dtype),
        in_specs=[SCALARS] + [ANY] * len(pieces),
        out_specs=WHOLE,
        scratch_shapes=[pltpu.SemaphoreType.DMA((32,))],
        compiler_params=pltpu.CompilerParams(vmem_limit_bytes=VMEM_GRANT),
        cost_estimate=pl.CostEstimate(flops=0, bytes_accessed=3 * size, transcendentals=0),
        name=name,
    )(where, *pieces)


def panel_moves(where, pieces, panel):
    width = pieces[0].shape[3]
    for dx in range(4):
        for dc in range(2):
            for dyl in range(2):
                place = where[((dx & 1) * 2 + dyl) * 2 + dc]
                for dh in range(2):
                    yield (
                        pieces[dx * 2 + dc].at[dyl, dh],
                        panel.at[place, dx >> 1, :, pl.ds(dh * width, width)],
                    )


def slab_moves(where, pieces, panel):
    width = pieces[0].shape[2]
    for k in range(8):
        for dx2 in range(2):
            for dh in range(2):
                yield (
                    pieces[0].at[where[(k * 2 + dx2) * 2 + dh]],
                    panel.at[k, dx2, :, pl.ds(dh * width, width)],
                )


def stack_moves(where, pieces, panel):
    rows = pieces[0].shape[0]
    for n, piece in enumerate(pieces):
        yield piece, panel.at[pl.ds(n * rows, rows)]


def roll_moves(where, pieces, panel):
    for k in range(8):
        yield pieces[0].at[where[k]], panel.at[k]


def head(where, pieces, weights):
    tokens, width = pieces[0].shape[2:]
    half = weights.shape[0]

    def kernel(where_ref, *refs):
        weights_ref, panel, outs, sems = refs[8], refs[9], refs[10:12], refs[12]
        copies = [
            pltpu.make_async_copy(source, place, sems.at[n])
            for n, (source, place) in enumerate(panel_moves(where_ref, refs[:8], panel))
        ]
        for copy in copies:
            copy.start()
        for copy in copies:
            copy.wait()
        for out, k in zip(outs, (4, 5)):
            rows = panel[k].reshape(2 * tokens, 2 * width)
            out[...] = dot(rows, weights_ref[...], 1, 1).astype(BF)

    return pl.pallas_call(
        kernel,
        out_shape=[jax.ShapeDtypeStruct((8, 2, tokens, 2 * width), BF)]
        + [jax.ShapeDtypeStruct((2 * tokens, half), BF)] * 2,
        in_specs=[SCALARS] + [ANY] * 8 + [WHOLE],
        out_specs=[WHOLE] * 3,
        scratch_shapes=[pltpu.SemaphoreType.DMA((32,))],
        compiler_params=pltpu.CompilerParams(vmem_limit_bytes=VMEM_GRANT),
        cost_estimate=pl.CostEstimate(flops=16 * tokens * width * half, bytes_accessed=96 * tokens * width, transcendentals=0),
        name="head",
    )(where, *pieces, weights)


def spread(where, pieces):
    tokens, width = pieces[0].shape[0] // 2, pieces[0].shape[1]

    def kernel(where_ref, *refs):
        sums, parts, total = refs[:8], refs[8:12], refs[12]
        for n in range(8):
            total[where_ref[n]] = sums[n][...]
        for d in range(4):
            for dyl in range(2):
                for dc in range(2):
                    part = total[((d & 1) * 2 + dyl) * 2 + dc, pl.ds((d >> 1) * tokens, tokens)]
                    parts[d][dyl, dc] = part.astype(parts[d].dtype)

    return pl.pallas_call(
        kernel,
        out_shape=[jax.ShapeDtypeStruct((2, 2, tokens, width), BF if d else F32) for d in range(4)],
        in_specs=[SCALARS] + [WHOLE] * 8,
        out_specs=[WHOLE] * 4,
        scratch_shapes=[pltpu.VMEM((8, 2 * tokens, width), F32)],
        compiler_params=pltpu.CompilerParams(vmem_limit_bytes=VMEM_GRANT),
        cost_estimate=pl.CostEstimate(flops=0, bytes_accessed=104 * tokens * width, transcendentals=0),
        name="spread",
    )(where, *pieces)


def local(inputs, out_grad, preact, w_in, w_out):
    h, z, x = lax.axis_index("h"), lax.axis_index("z"), lax.axis_index("x")
    yl, c = lax.axis_index("yl"), lax.axis_index("c")
    low = (x & 1) * 4 + yl * 2 + c
    ks = jnp.arange(8, dtype=jnp.int32)
    place_of = ((ks ^ low) - z) & 7
    half = preact.shape[1] // 2
    tokens, width = out_grad.shape

    def halves(a, axis):
        return (
            lax.dynamic_slice_in_dim(a, h * half, half, axis=axis),
            lax.dynamic_slice_in_dim(a, (1 - h) * half, half, axis=axis),
        )

    hidden = gelu_value(preact.astype(F32)).astype(BF)
    hidden_slab = lax.all_gather(hidden, "z", axis=0)
    slab = lax.all_gather(after(inputs, hidden), ("h", "x", "yl", "c"), axis=0)
    pre_own, pre_send = halves(preact, 1)
    pre_recv = swap_h(pre_send)
    y1, y2, y3 = swap_y(out_grad, 1), swap_y(out_grad, 2), swap_y(out_grad, 3)
    own = jnp.stack([jnp.stack([out_grad, y2]), jnp.stack([y1, y3])])
    wo_own, wo_send = halves(w_out, 0)
    wi_own, wi_send = halves(w_in, 1)
    wo_send, wi_send = after(wo_send, own), after(wi_send, own)
    by_x = [own] + [swap_x(own, d) for d in (1, 2, 3)]
    grad_pieces = []
    for piece in by_x:
        grad_pieces += [piece, swap_c(piece)]
    w_out2 = jnp.concatenate([wo_own, swap_h(wo_send)], axis=1)

    first_own = h == (x >> 1)

    wi_other = swap_h(wi_send)

    panel, run_up, run_down = head(place_of, grad_pieces, w_out2)
    panel_all = panel.reshape(16 * tokens, 2 * width)
    parts = dot(panel_all, w_out2, 1, 1).reshape(8, 2 * tokens, half)

    def add(part, got):
        return (part + got.astype(F32)).astype(BF)

    run_up, run_down, wi_other = together(run_up, run_down, wi_other)
    run_up, run_down = up(run_up), down(run_down)
    w_in_keep = jnp.where(c == 0, wi_own, wi_other)
    w_in_send = jnp.where(c == 0, wi_other, wi_own)
    run_up, run_down, pre_recv = together(add(parts[3], run_up), add(parts[6], run_down), pre_recv)
    slope = gelu_slope(
        jnp.where(
            first_own, jnp.concatenate([pre_own, pre_recv], axis=0), jnp.concatenate([pre_recv, pre_own], axis=0)
        ).astype(F32)
    )
    run_up, run_down = up(run_up), down(run_down)
    run_up, run_down = together(add(parts[2], run_up), add(parts[7], run_down))
    run_up, run_down = up(run_up), down(run_down)
    hidden_all = assemble(roll_moves, (z + ks) & 7, [hidden_slab], (8, tokens, 2 * half), "hidden_panel")
    hidden_all = hidden_all.reshape(8 * tokens, 2 * half)
    grad_half = lax.dynamic_index_in_dim(panel, jnp.where(first_own, 0, 1), axis=1, keepdims=False)
    grad_half = grad_half.reshape(8 * tokens, 2 * width)
    run_up = up(add(parts[1], run_up))
    run_up, run_down, hidden_all, grad_half, slope, w_in_keep, w_in_send = together(
        run_up, run_down, hidden_all, grad_half, slope, w_in_keep, w_in_send
    )
    total = parts[0] + run_down.astype(F32) + run_up.astype(F32)

    g = [None] * 8
    g[0] = (total * slope).astype(BF)

    def both_cores(chunk):
        got = swap_c(dot(chunk, w_in_send, 1, 1).astype(BF))
        return dot(chunk, w_in_keep, 1, 1) + got.astype(F32)

    sums = [None] * 8
    g[7], g[1] = up(g[0]), down(g[0])
    wo_other = dot(hidden_all, grad_half[:, width:], 0, 0).astype(BF)
    wo_mine = dot(hidden_all, grad_half[:, :width], 0, 0)
    g[7], g[1], wo_other, wo_mine = together(g[7], g[1], wo_other, wo_mine)
    g[6], g[2] = up(g[7]), down(g[1])
    sums[0], sums[1], sums[7] = [both_cores(after(g[k], g[7])) for k in (0, 1, 7)]
    g[6], g[2], sums[0], sums[1], sums[7] = together(g[6], g[2], sums[0], sums[1], sums[7])
    g[5], g[3] = up(g[6]), down(g[2])
    sums[2], sums[6] = both_cores(g[2]), both_cores(g[6])
    g[5], sums[2], sums[6] = together(g[5], sums[2], sums[6])
    g[4] = up(g[5])
    sums[3], sums[5] = both_cores(g[3]), both_cores(g[5])
    n = jnp.arange(32, dtype=jnp.int32)
    k = jnp.array([0, 1, 2, 3, 5, 6, 7, 4], jnp.int32)[n >> 2]
    owner = (((n & 1) ^ h) * 2 + (((n >> 1) & 1) ^ (x >> 1))) * 8 + ((z + k) & 7)
    slab = after(slab, g[5])
    wo_other = swap_h(after(wo_other, slab))
    input_all = assemble(slab_moves, owner, [slab], (8, 2, tokens, 2 * width), "input_panel")
    input_all = input_all.reshape(16 * tokens, 2 * width)
    early = 14 * tokens
    grad_early = assemble(stack_moves, ks, g[:4] + g[5:], (early, half), "preact_panel")
    wi_send = dot(input_all[:early, width:], grad_early, 0, 0)
    g[4], sums[3], sums[5], wi_send = together(g[4], sums[3], sums[5], wi_send)
    sums[4] = both_cores(g[4])
    wi_send = (wi_send + dot(input_all[early:, width:], g[4], 0, 0)).astype(BF)
    wi_other = swap_h(wi_send)
    sums[4] = after(sums[4], wi_send)
    slot_of = low ^ ((z + ks) & 7)
    by_x, *others = spread(slot_of, sums)
    others = [swap_x(others[d - 1], d) for d in (1, 2, 3)]

    wo_other, g[4], grad_early = after(wo_other, by_x), after(g[4], by_x), after(grad_early, by_x)
    wi_mine = dot(input_all[:early, :width], grad_early, 0, 0) + dot(input_all[early:, :width], g[4], 0, 0)
    w_out_grad = wo_mine + wo_other.astype(F32)
    others[1], wi_mine, w_out_grad = together(others[1], wi_mine, w_out_grad)

    for part in others:
        by_x = by_x + part.astype(F32)
    to_first = [(i, i ^ 2) if i % 2 == 0 else (i, i ^ 6) for i in range(8)]
    to_second = [(i, i ^ 4) for i in range(1, 8, 2)]
    moved, wi_other = together(by_x.astype(BF), wi_other)
    got = lax.ppermute(moved[1], ("h", "yl", "c"), to_first).astype(F32)
    got_second = lax.ppermute(moved[0], ("h", "yl", "c"), to_second).astype(F32)
    by_y = got + jnp.where(c == 0, by_x[0], got_second)
    by_y = by_y[0] + swap_c(by_y[1])
    input_grad = by_y.astype(BF)
    w_in_grad = jnp.where(
        h == 0,
        jnp.concatenate([wi_mine, wi_other.astype(F32)], axis=1),
        jnp.concatenate([wi_other.astype(F32), wi_mine], axis=1),
    )
    return input_grad, w_in_grad, w_out_grad


def solution(mesh):
    fine = Mesh(mesh.devices.reshape(2, RING, 4, 2, 2), ("h", "z", "x", "yl", "c"))
    col, row = ("x", "yl", "c"), ("h", "z")
    in_specs = (P(col, row), P(col, row), P(row, col), P(row, col), P(col, row))
    out_specs = (P(col, row), P(row, col), P(col, row))
    return jax.shard_map(local, mesh=fine, in_specs=in_specs, out_specs=out_specs, check_vma=False)
```

```python
import functools

import jax
import jax.numpy as jnp
from jax import lax
from jax.experimental import pallas as pl
from jax.experimental.pallas import tpu as pltpu
from jax.sharding import Mesh, PartitionSpec as P

BF = jnp.bfloat16
F32 = jnp.float32
RING = 8
VMEM_GRANT = 48 * 1024 * 1024


def gelu_value(z):
    inner = 0.7978845608 * (z + 0.044715 * z * z * z)
    return 0.5 * z * (1.0 + jnp.tanh(inner))


def gelu_slope(z):
    inner = 0.7978845608 * (z + 0.044715 * z * z * z)
    tangent = jnp.tanh(inner)
    return 0.5 * (1.0 + tangent) + 0.5 * z * (1.0 - tangent * tangent) * 0.7978845608 * (
        1.0 + 3.0 * 0.044715 * z * z
    )


def up(a):
    return lax.ppermute(a, "z", [(i, (i + 1) % RING) for i in range(RING)])


def down(a):
    return lax.ppermute(a, "z", [(i, (i - 1) % RING) for i in range(RING)])


def swap_h(a):
    return lax.ppermute(a, "h", [(0, 1), (1, 0)])


def swap_c(a):
    return lax.ppermute(a, "c", [(0, 1), (1, 0)])


def swap_x(a, d):
    return lax.ppermute(a, "x", [(i, i ^ d) for i in range(4)])


def swap_y(a, d):
    return lax.ppermute(a, ("h", "yl"), [(i, i ^ d) for i in range(4)])


def together(*arrays):
    return lax.optimization_barrier(arrays)


def after(a, *others):
    return lax.optimization_barrier((a,) + others)[0]


def dot(a, b, ca, cb):
    return lax.dot_general(a, b, (((ca,), (cb,)), ((), ())), preferred_element_type=F32)


ANY = pl.BlockSpec(memory_space=pl.ANY)
SCALARS = pl.BlockSpec(memory_space=pltpu.SMEM)
WHOLE = pl.BlockSpec(memory_space=pltpu.VMEM)


def assemble(moves, where, pieces, shape, name):
    def kernel(where_ref, *refs):
        panel, sems = refs[-2], refs[-1]
        copies = [
            pltpu.make_async_copy(source, place, sems.at[n])
            for n, (source, place) in enumerate(moves(where_ref, refs[:-2], panel))
        ]
        for copy in copies:
            copy.start()
        for copy in copies:
            copy.wait()

    size = pieces[0].dtype.itemsize
    for length in shape:
        size *= length
    return pl.pallas_call(
        kernel,
        out_shape=jax.ShapeDtypeStruct(shape, pieces[0].dtype),
        in_specs=[SCALARS] + [ANY] * len(pieces),
        out_specs=WHOLE,
        scratch_shapes=[pltpu.SemaphoreType.DMA((32,))],
        compiler_params=pltpu.CompilerParams(vmem_limit_bytes=VMEM_GRANT),
        cost_estimate=pl.CostEstimate(flops=0, bytes_accessed=3 * size, transcendentals=0),
        name=name,
    )(where, *pieces)


def panel_moves(where, pieces, panel):
    width = panel.shape[3] // 2
    held = (((0, 0),), ((0, 1),), ((1, 0),), ((3, 1),), ((3, 0), (2, 0)), ((1, 1), (2, 1)))
    for dc in range(2):
        for piece, blocks in zip(pieces[dc::2], held):
            for n, (dx, dyl) in enumerate(blocks):
                place = where[((dx & 1) * 2 + dyl) * 2 + dc]
                for dh in range(2):
                    yield piece.at[n, dh], panel.at[place, dx >> 1, :, pl.ds(dh * width, width)]


def slab_moves(where, pieces, panel):
    width = pieces[0].shape[2]
    for k in range(8):
        for dx2 in range(2):
            for dh in range(2):
                yield (
                    pieces[0].at[where[(k * 2 + dx2) * 2 + dh]],
                    panel.at[k, dx2, :, pl.ds(dh * width, width)],
                )


def stack_moves(where, pieces, panel):
    rows = pieces[0].shape[0]
    for n, piece in enumerate(pieces):
        yield piece, panel.at[pl.ds(n * rows, rows)]


def roll_moves(where, pieces, panel):
    for k in range(8):
        yield pieces[0].at[where[k]], panel.at[k]


def head(where, pieces, weights):
    tokens, width = pieces[0].shape[2:]
    half = weights.shape[0]
    count = len(pieces)

    def kernel(where_ref, *refs):
        weights_ref, panel, outs, sems = refs[count], refs[count + 1], refs[count + 2 : count + 4], refs[count + 4]
        copies = [
            pltpu.make_async_copy(source, place, sems.at[n])
            for n, (source, place) in enumerate(panel_moves(where_ref, refs[:count], panel))
        ]
        for copy in copies:
            copy.start()
        for copy in copies:
            copy.wait()
        for out, k in zip(outs, (4, 5)):
            rows = panel[k].reshape(2 * tokens, 2 * width)
            out[...] = dot(rows, weights_ref[...], 1, 1).astype(BF)

    return pl.pallas_call(
        kernel,
        out_shape=[jax.ShapeDtypeStruct((8, 2, tokens, 2 * width), BF)]
        + [jax.ShapeDtypeStruct((2 * tokens, half), BF)] * 2,
        in_specs=[SCALARS] + [ANY] * count + [WHOLE],
        out_specs=[WHOLE] * 3,
        scratch_shapes=[pltpu.SemaphoreType.DMA((32,))],
        compiler_params=pltpu.CompilerParams(vmem_limit_bytes=VMEM_GRANT),
        cost_estimate=pl.CostEstimate(flops=16 * tokens * width * half, bytes_accessed=96 * tokens * width, transcendentals=0),
        name="head",
    )(where, *pieces, weights)


def spread(where, pieces):
    tokens, width = pieces[0].shape[0] // 2, pieces[0].shape[1]

    def kernel(where_ref, *refs):
        sums, parts, total = refs[:8], refs[8:12], refs[12]
        for n in range(8):
            total[where_ref[n]] = sums[n][...]
        for d in range(4):
            for dyl in range(2):
                for dc in range(2):
                    part = total[((d & 1) * 2 + dyl) * 2 + dc, pl.ds((d >> 1) * tokens, tokens)]
                    parts[d][dyl, dc] = part.astype(parts[d].dtype)

    return pl.pallas_call(
        kernel,
        out_shape=[jax.ShapeDtypeStruct((2, 2, tokens, width), BF if d else F32) for d in range(4)],
        in_specs=[SCALARS] + [WHOLE] * 8,
        out_specs=[WHOLE] * 4,
        scratch_shapes=[pltpu.VMEM((8, 2 * tokens, width), F32)],
        compiler_params=pltpu.CompilerParams(vmem_limit_bytes=VMEM_GRANT),
        cost_estimate=pl.CostEstimate(flops=0, bytes_accessed=104 * tokens * width, transcendentals=0),
        name="spread",
    )(where, *pieces)


def local(inputs, out_grad, preact, w_in, w_out):
    h, z, x = lax.axis_index("h"), lax.axis_index("z"), lax.axis_index("x")
    yl, c = lax.axis_index("yl"), lax.axis_index("c")
    low = (x & 1) * 4 + yl * 2 + c
    ks = jnp.arange(8, dtype=jnp.int32)
    place_of = ((ks ^ low) - z) & 7
    half = preact.shape[1] // 2
    tokens, width = out_grad.shape

    def halves(a, axis):
        return (
            lax.dynamic_slice_in_dim(a, h * half, half, axis=axis),
            lax.dynamic_slice_in_dim(a, (1 - h) * half, half, axis=axis),
        )

    hidden = gelu_value(preact.astype(F32)).astype(BF)
    hidden_slab = lax.all_gather(hidden, "z", axis=0)
    slab = lax.all_gather(after(inputs, hidden), ("h", "x", "yl", "c"), axis=0)
    pre_own, pre_send = halves(preact, 1)
    pre_recv = swap_h(pre_send)
    y1, y2, y3 = swap_y(out_grad, 1), swap_y(out_grad, 2), swap_y(out_grad, 3)
    own_a, own = jnp.stack([out_grad, y2])[None], jnp.stack([y1, y3])[None]
    wo_own, wo_send = halves(w_out, 0)
    wi_own, wi_send = halves(w_in, 1)
    wo_send, wi_send = after(wo_send, own), after(wi_send, own)
    one_a, one_b = swap_x(own_a, 1), swap_x(own, 3)
    two_a = swap_x(jnp.concatenate([own_a, one_a]), 3)
    two_b = swap_x(jnp.concatenate([own, one_b]), 1)
    grad_pieces = []
    for piece in (own_a, own, one_a, one_b, two_a, two_b):
        grad_pieces += [piece, swap_c(piece)]
    w_out2 = jnp.concatenate([wo_own, swap_h(wo_send)], axis=1)

    first_own = h == (x >> 1)

    wi_other = swap_h(wi_send)

    panel, run_up, run_down = head(place_of, grad_pieces, w_out2)
    panel_all = panel.reshape(16 * tokens, 2 * width)
    parts = dot(panel_all, w_out2, 1, 1).reshape(8, 2 * tokens, half)

    def add(part, got):
        return (part + got.astype(F32)).astype(BF)

    run_up, run_down, wi_other = together(run_up, run_down, wi_other)
    run_up, run_down = up(run_up), down(run_down)
    w_in_keep = jnp.where(c == 0, wi_own, wi_other)
    w_in_send = jnp.where(c == 0, wi_other, wi_own)
    run_up, run_down = together(add(parts[3], run_up), add(parts[6], run_down))
    run_up, run_down = up(run_up), down(run_down)
    run_up, run_down, pre_recv = together(add(parts[2], run_up), add(parts[7], run_down), pre_recv)
    slope = gelu_slope(
        jnp.where(
            first_own, jnp.concatenate([pre_own, pre_recv], axis=0), jnp.concatenate([pre_recv, pre_own], axis=0)
        ).astype(F32)
    )
    run_up, run_down = up(run_up), down(run_down)
    hidden_all = assemble(roll_moves, (z + ks) & 7, [hidden_slab], (8, tokens, 2 * half), "hidden_panel")
    hidden_all = hidden_all.reshape(8 * tokens, 2 * half)
    grad_half = lax.dynamic_index_in_dim(panel, jnp.where(first_own, 0, 1), axis=1, keepdims=False)
    grad_half = grad_half.reshape(8 * tokens, 2 * width)
    run_up = up(add(parts[1], run_up))
    run_up, run_down, hidden_all, grad_half, slope, w_in_keep, w_in_send = together(
        run_up, run_down, hidden_all, grad_half, slope, w_in_keep, w_in_send
    )
    total = parts[0] + run_down.astype(F32) + run_up.astype(F32)

    g = [None] * 8
    g[0] = (total * slope).astype(BF)

    def both_cores(chunk):
        got = swap_c(dot(chunk, w_in_send, 1, 1).astype(BF))
        return dot(chunk, w_in_keep, 1, 1) + got.astype(F32)

    sums = [None] * 8
    g[7], g[1] = up(g[0]), down(g[0])
    wo_other = dot(hidden_all, grad_half[:, width:], 0, 0).astype(BF)
    wo_mine = dot(hidden_all, grad_half[:, :width], 0, 0)
    g[7], g[1], wo_other, wo_mine = together(g[7], g[1], wo_other, wo_mine)
    g[6], g[2] = up(g[7]), down(g[1])
    sums[0], sums[1], sums[7] = [both_cores(after(g[k], g[7])) for k in (0, 1, 7)]
    g[6], g[2], sums[0], sums[1], sums[7] = together(g[6], g[2], sums[0], sums[1], sums[7])
    g[5], g[3] = up(g[6]), down(g[2])
    sums[2], sums[6] = both_cores(g[2]), both_cores(g[6])
    g[5], sums[2], sums[6] = together(g[5], sums[2], sums[6])
    g[4] = up(g[5])
    sums[3], sums[5] = both_cores(g[3]), both_cores(g[5])
    n = jnp.arange(32, dtype=jnp.int32)
    k = jnp.array([0, 1, 2, 3, 5, 6, 7, 4], jnp.int32)[n >> 2]
    owner = (((n & 1) ^ h) * 2 + (((n >> 1) & 1) ^ (x >> 1))) * 8 + ((z + k) & 7)
    slab = after(slab, g[5])
    wo_other = swap_h(after(wo_other, slab))
    input_all = assemble(slab_moves, owner, [slab], (8, 2, tokens, 2 * width), "input_panel")
    input_all = input_all.reshape(16 * tokens, 2 * width)
    early = 14 * tokens
    grad_early = assemble(stack_moves, ks, g[:4] + g[5:], (early, half), "preact_panel")
    wi_send = dot(input_all[:early, width:], grad_early, 0, 0)
    g[4], sums[3], sums[5], wi_send = together(g[4], sums[3], sums[5], wi_send)
    sums[4] = both_cores(g[4])
    wi_send = (wi_send + dot(input_all[early:, width:], g[4], 0, 0)).astype(BF)
    wi_other = swap_h(wi_send)
    sums[4] = after(sums[4], wi_send)
    slot_of = low ^ ((z + ks) & 7)
    by_x, *others = spread(slot_of, sums)
    others = [swap_x(others[d - 1], d) for d in (1, 2, 3)]

    wo_other, g[4], grad_early = after(wo_other, by_x), after(g[4], by_x), after(grad_early, by_x)
    wi_mine = dot(input_all[:early, :width], grad_early, 0, 0) + dot(input_all[early:, :width], g[4], 0, 0)
    w_out_grad = wo_mine + wo_other.astype(F32)
    others[1], wi_mine, w_out_grad = together(others[1], wi_mine, w_out_grad)

    for part in others:
        by_x = by_x + part.astype(F32)
    to_first = [(i, i ^ 2) if i % 2 == 0 else (i, i ^ 6) for i in range(8)]
    to_second = [(i, i ^ 4) for i in range(1, 8, 2)]
    moved, wi_other = together(by_x.astype(BF), wi_other)
    got = lax.ppermute(moved[1], ("h", "yl", "c"), to_first).astype(F32)
    got_second = lax.ppermute(moved[0], ("h", "yl", "c"), to_second).astype(F32)
    by_y = got + jnp.where(c == 0, by_x[0], got_second)
    by_y = by_y[0] + swap_c(by_y[1])
    input_grad = by_y.astype(BF)
    w_in_grad = jnp.where(
        h == 0,
        jnp.concatenate([wi_mine, wi_other.astype(F32)], axis=1),
        jnp.concatenate([wi_other.astype(F32), wi_mine], axis=1),
    )
    return input_grad, w_in_grad, w_out_grad


def solution(mesh):
    fine = Mesh(mesh.devices.reshape(2, RING, 4, 2, 2), ("h", "z", "x", "yl", "c"))
    col, row = ("x", "yl", "c"), ("h", "z")
    in_specs = (P(col, row), P(col, row), P(row, col), P(row, col), P(col, row))
    out_specs = (P(col, row), P(row, col), P(col, row))
    return jax.shard_map(local, mesh=fine, in_specs=in_specs, out_specs=out_specs, check_vma=False)
```
